32 devices in a mesh: bead: 8 (over y, x, core), atom: 4 (over z).
Axes of the slice: x: 2, y: 2, z: 4, core: 2. Of those that a mesh axis runs over, the one named last changes fastest.
Arguments:
- positions: float32 [3, 8, 1024], P(None, 'bead', 'atom'), may hold values from -1 to 11, as said below
- velocities: float32 [3, 8, 1024], P(None, 'bead', 'atom'), may hold values from -3 to 3
- forces_now: float32 [3, 8, 1024], P(None, 'bead', 'atom'), may hold values from -18 to 18
- masses: float32 [1024], P('atom'), may hold values from 1 to 16
- features: bfloat16 [8, 256, 1024], P('bead', None, 'atom'), may hold values from -6 to 6
- tile_blocks: int32 [8, 9], P('atom'), may hold values from 0 to 7, as said below
- block_slots: int32 [1024], P('atom'), may hold values from 0 to 1023, as said below
- w_basis: bfloat16 [64, 32], replicated, may hold values from -1 to 1
- w_feat: bfloat16 [64, 256], replicated, may hold values from -0.375 to 0.375
- hidden_bias: float32 [64], replicated, may hold values from -5 to 5
- w_out: float32 [64], replicated, may hold values from -0.03 to 0.03
Outputs:
- positions_next: float32 [3, 8, 1024], P(None, 'bead', 'atom')
- velocities_next: float32 [3, 8, 1024], P(None, 'bead', 'atom')
- forces_next: float32 [3, 8, 1024], P(None, 'bead', 'atom')
The draws below stay inside these ranges and needn't reach their ends.
Inputs may be any that keep to these rules, and one draw needn't show every extreme that they name: `tile_blocks`: every entry of row k is one of the blocks k - 4 to k + 4, counted cyclically over the 8 blocks; blocks k - 4 and k + 4 are always named; the other entries may repeat; the order is drawn for each row. `block_slots`: the entries j * 256 to (j + 1) * 256 - 1 are a permutation of the atom numbers j * 256 to (j + 1) * 256 - 1. `positions`: the beads of one atom lie within 0.06, in each coordinate, of a common centre whose first two coordinates lie in [0, 2.9) and whose third lies in [0.15 k, 0.15 (k + 1)), k the block of the atom's slot.
All inputs are finite; a program needn't handle non-finite values.
Results may differ from the reference program's by a relative error of at most 0.0003.
Values may be sent and summed in bfloat16 or wider, within the bound.
A program may use at most 128 MiB of HBM per device.

```python
import math
import jax
import jax.numpy as jnp
from jax import lax

TILE = 128
NB = 32
HID = 64
FEAT = 256
TPB = 9
BLK_DEV = 2
ATOM_DEV = 256
BLOCKS = 8
ATOMS = 1024
BEADS = 8


def slot_layout(key):
    stretches = ATOMS // ATOM_DEV
    scores = jax.random.randint(key, (stretches, ATOM_DEV), 0, 1 << 16) * ATOM_DEV + jnp.arange(ATOM_DEV, dtype=jnp.int32)[None, :]
    return jnp.argsort(scores, axis=1).astype(jnp.int32)


def draw_block_slots(key, part):
    local_order = slot_layout(jax.random.fold_in(key, 11))
    stretch_base = jnp.arange(ATOMS // ATOM_DEV, dtype=jnp.int32)[:, None] * ATOM_DEV
    return (local_order + stretch_base).reshape(ATOMS).astype(jnp.int32)


def draw_positions(key, part):
    local_order = slot_layout(jax.random.fold_in(key, 11))
    slot_of = jnp.argsort(local_order, axis=1).astype(jnp.int32)
    stretch_ids = jnp.arange(ATOMS // ATOM_DEV, dtype=jnp.int32)[:, None]
    block_of = (stretch_ids * BLK_DEV + slot_of // TILE).reshape(ATOMS).astype(jnp.float32)
    key_one, key_two, key_three = jax.random.split(jax.random.fold_in(key, 23), 3)
    plane_xy = jax.random.uniform(key_one, (2, ATOMS), jnp.float32) * 2.9
    height = (block_of + jax.random.uniform(key_two, (ATOMS,), jnp.float32)) * 0.15
    centre_pos = jnp.concatenate([plane_xy, height[None, :]], axis=0)
    bead_noise = jnp.clip(jax.random.normal(key_three, (3, BEADS, ATOMS), jnp.float32) * 0.015, -0.06, 0.06)
    return (centre_pos[:, None, :] + bead_noise).astype(jnp.float32)


def draw_tile_blocks(key, part):
    key_one, key_two = jax.random.split(jax.random.fold_in(key, 37), 2)
    fixed_low = jnp.full((BLOCKS, 1), -4, jnp.int32)
    fixed_high = jnp.full((BLOCKS, 1), 4, jnp.int32)
    drawn = jax.random.randint(key_one, (BLOCKS, TPB - 2), -4, 5).astype(jnp.int32)
    values = jnp.concatenate([fixed_low, fixed_high, drawn], axis=1)
    scores = jax.random.randint(key_two, (BLOCKS, TPB), 0, 1 << 16) * TPB + jnp.arange(TPB, dtype=jnp.int32)[None, :]
    order = jnp.argsort(scores, axis=1).astype(jnp.int32)
    shuffled = jnp.take_along_axis(values, order, axis=1)
    row_ids = jnp.arange(BLOCKS, dtype=jnp.int32)[:, None]
    return ((row_ids + shuffled) % BLOCKS).astype(jnp.int32)


def levels(key, shape, cuts, smallest, largest):
    factor_of, own = 1.0, jax.random.fold_in(key, 6)
    for position, blocks in cuts:
        steps = jnp.exp(jax.random.uniform(jax.random.fold_in(own, position), (blocks,), jnp.float32, smallest / len(cuts), largest / len(cuts)))
        factor_of = factor_of * jnp.repeat(steps, shape[position] // blocks).reshape([-1 if axis == position else 1 for axis in range(len(shape))])
    return factor_of


def noise(own_key, dims, deviation, bound, shards=(), kind=jnp.bfloat16):
    array = jax.random.normal(own_key, dims, jnp.float32) * deviation
    if len(shards) > 0:
        array = levels(own_key, dims, shards, -0.22, 0.18) * array
    return jnp.clip(array, min=-bound, max=bound).astype(kind)


def setup_inputs(seed: int = 0) -> dict:
    seeds = jax.random.split(jax.random.key(seed), 12)
    positions = draw_positions(jax.random.fold_in(seeds[11], 71), 0)
    velocities = noise(seeds[1], (3, BEADS, ATOMS), 0.5, 3.0, ((1, 8), (2, 4)), jnp.float32)
    forces_now = noise(seeds[2], (3, BEADS, ATOMS), 3.0, 18.0, ((1, 8), (2, 4)), jnp.float32)
    masses = jnp.clip(jnp.exp(math.log(16.0) - 2.7725887 * jax.random.uniform(seeds[3], (ATOMS,), jnp.float32) ** levels(seeds[3], (ATOMS,), ((0, 4),), -0.2, 0.2)), 1.0, 16.0)
    features = noise(seeds[4], (BEADS, FEAT, ATOMS), 1.0, 6.0, ((0, 8), (2, 4)))
    tile_blocks = draw_tile_blocks(jax.random.fold_in(seeds[11], 71), 0)
    block_slots = draw_block_slots(jax.random.fold_in(seeds[11], 71), 0)
    w_basis = noise(seeds[7], (HID, NB), NB ** -0.5, 1.0)
    w_feat = noise(seeds[8], (HID, FEAT), FEAT ** -0.5, 0.375)
    hidden_bias = noise(seeds[9], (HID,), 1.0, 5.0, (), jnp.float32)
    w_out = noise(seeds[10], (HID,), 0.005, 0.03, (), jnp.float32)
    return {"positions": positions, "velocities": velocities, "forces_now": forces_now, "masses": masses, "features": features, "tile_blocks": tile_blocks, "block_slots": block_slots, "w_basis": w_basis, "w_feat": w_feat, "hidden_bias": hidden_bias, "w_out": w_out}


LAYER_WIDTH = 0.15
SIDE_LENGTH = 2.9
CUTOFF = 0.6
BASIS_SHARPNESS = 355.0
SOFTEN = 0.0001
TIME_STEP = 0.1
OMEGA_SQ = 100.0
rows_per_turn = 16

def pair_terms(q_rows, p_rows, q_cols, p_cols, self_mask, w_basis, hidden_bias, w_out, box_depth):
    box_size = jnp.stack([jnp.float32(SIDE_LENGTH), jnp.float32(SIDE_LENGTH), jnp.float32(box_depth)]).reshape(3, 1, 1)
    displace = q_cols[:, None, :] - q_rows[:, :, None]
    displace = displace - box_size * jnp.floor(displace / box_size + 0.5)
    dist_sq = lax.optimization_barrier(jnp.sum(displace * displace, axis=0))
    distance = jnp.sqrt(dist_sq + SOFTEN)
    inner_part = jnp.maximum(1.0 - dist_sq / (CUTOFF * CUTOFF), 0.0)
    smooth = inner_part * inner_part
    smooth_slope = -2.0 * inner_part / (CUTOFF * CUTOFF)
    basis_count = w_basis.shape[1]
    centres = (CUTOFF * (jnp.arange(basis_count, dtype=jnp.float32) + 0.5) / basis_count).reshape(basis_count, 1, 1)
    offset = distance[None] - centres
    basis_vals = jnp.exp(-BASIS_SHARPNESS * offset * offset)
    row_count, col_count = dist_sq.shape
    basis_half = basis_vals.astype(jnp.bfloat16).reshape(basis_count, row_count * col_count)
    pre_act = jnp.dot(w_basis, basis_half, preferred_element_type=jnp.float32).reshape(-1, row_count, col_count)
    pre_act = pre_act + p_rows.astype(jnp.float32)[:, :, None] + p_cols.astype(jnp.float32)[:, None, :] + hidden_bias[:, None, None]
    activation = jnp.tanh(pre_act)
    energy = lax.optimization_barrier(jnp.sum(w_out[:, None, None] * activation, axis=0))
    back_grad = (w_out[:, None, None] * (1.0 - activation * activation)).astype(jnp.bfloat16).reshape(-1, row_count * col_count)
    grad_basis = lax.dot_general(w_basis, back_grad, (((0,), (0,)), ((), ())), preferred_element_type=jnp.float32).reshape(basis_count, row_count, col_count)
    dbasis = -BASIS_SHARPNESS * offset * basis_vals / distance[None]
    de_ds = smooth_slope * energy + smooth * lax.optimization_barrier(jnp.sum(grad_basis * dbasis, axis=0))
    de_ds = jnp.where(self_mask, 0.0, de_ds)
    return lax.optimization_barrier(jnp.sum(2.0 * de_ds[None] * displace, axis=2))

def block_forces(pos_all, proj_all, own_block, sources, w_basis, hidden_bias, w_out, box_depth):
    start = (own_block * TILE).astype(jnp.int32)
    pos_own = lax.dynamic_slice_in_dim(pos_all, start, TILE, 1)
    proj_own = lax.dynamic_slice_in_dim(proj_all, start, TILE, 1)
    tile_count = sources.shape[0]
    q_cols = jnp.concatenate([lax.dynamic_slice_in_dim(pos_all, (sources[k] * TILE).astype(jnp.int32), TILE, 1) for k in range(tile_count)], axis=1)
    p_cols = jnp.concatenate([lax.dynamic_slice_in_dim(proj_all, (sources[k] * TILE).astype(jnp.int32), TILE, 1) for k in range(tile_count)], axis=1)
    col_source = jnp.repeat(sources.astype(jnp.int32), TILE)
    col_local = jnp.tile(jnp.arange(TILE, dtype=jnp.int32), tile_count)
    row_ids = jnp.arange(rows_per_turn, dtype=jnp.int32)
    pieces = []
    for group_idx in range(TILE // rows_per_turn):
        low = group_idx * rows_per_turn
        q_rows = pos_own[:, low:low + rows_per_turn]
        p_rows = proj_own[:, low:low + rows_per_turn]
        self_mask = (col_source[None, :] == own_block) & (row_ids[:, None] + low == col_local[None, :])
        pieces.append(pair_terms(q_rows, p_rows, q_cols, p_cols, self_mask, w_basis, hidden_bias, w_out, box_depth))
    return jnp.concatenate(pieces, axis=1)

def reference(positions, velocities, forces_now, masses, features, tile_blocks, block_slots, w_basis, w_feat, hidden_bias, w_out):
    half_vel = velocities + 0.5 * TIME_STEP * forces_now / masses
    moved_pos = positions + TIME_STEP * half_vel
    sorted_pos = moved_pos[:, :, block_slots]
    sorted_feat = features[:, :, block_slots]
    projected = lax.map(lambda feats: jnp.dot(w_feat, feats, preferred_element_type=jnp.float32).astype(jnp.bfloat16), sorted_feat)
    box_depth = BLOCKS * LAYER_WIDTH

    def bead_forces(pair_in):
        pos_bead, proj_bead = pair_in
        per_block = lax.map(lambda block_idx: block_forces(pos_bead, proj_bead, block_idx, tile_blocks[block_idx], w_basis, hidden_bias, w_out, box_depth), jnp.arange(BLOCKS, dtype=jnp.int32))
        return jnp.transpose(per_block, (1, 0, 2)).reshape(3, BLOCKS * TILE)
    pair_sorted = lax.map(bead_forces, (jnp.transpose(sorted_pos, (1, 0, 2)), projected))
    pair_sorted = jnp.transpose(pair_sorted, (1, 0, 2))
    pair_force = jnp.zeros_like(moved_pos).at[:, :, block_slots].set(pair_sorted)
    spring = -OMEGA_SQ * masses * (2.0 * moved_pos - jnp.roll(moved_pos, 1, axis=1) - jnp.roll(moved_pos, -1, axis=1))
    forces_next = pair_force + spring
    velocities_next = half_vel + 0.5 * TIME_STEP * forces_next / masses
    return (moved_pos, velocities_next, forces_next)
```

```python
import functools

import jax
import jax.numpy as jnp
from jax import lax
from jax.experimental import pallas as pl
from jax.experimental.pallas import tpu as pltpu
from jax.sharding import PartitionSpec as P

TILE = 128
LAYER_WIDTH = 0.15
SIDE_LENGTH = 2.9
CUTOFF = 0.6
BASIS_SHARPNESS = 355.0
SOFTEN = 0.0001
TIME_STEP = 0.1
OMEGA_SQ = 100.0
REACH_BLOCKS = 4
SLOT = 16
SEGS = TILE // SLOT
LROWS = TILE // SEGS
STACK = 4
MESH = pl.DeviceIdType.MESH
f32, bf16, i32 = jnp.float32, jnp.bfloat16, jnp.int32


def iota(shape, dim):
    return lax.broadcasted_iota(i32, shape, dim)


def dot(a, b, dims=((1,), (0,)), exact=False):
    return lax.dot_general(
        a,
        b,
        (dims, ((), ())),
        precision=lax.Precision.HIGHEST if exact else None,
        preferred_element_type=f32,
    )


def split3(x):
    hi = x.astype(bf16)
    rest = x - hi.astype(f32)
    mid = rest.astype(bf16)
    low = (rest - mid.astype(f32)).astype(bf16)
    return hi, mid, low


def window(blocks_here, shards):
    reach = (REACH_BLOCKS + blocks_here - 1) // blocks_here
    span = min(2 * reach + 1, shards)
    return span, -(span // 2)


def one_hot_slots(slots_ref, shard, atoms):
    local = slots_ref[...] - shard * atoms
    return jnp.where(iota((atoms, atoms), 0) == local, 1.0, 0.0)


def exchange_kernel(
    shards, beads, span, first,
    pos_ref, vel_ref, force_ref, mass_ref, feat_ref, slots_ref, w_feat_ref,
    rim_ref, state_ref,
    mine, sides, send_sems, recv_sems, bead_send, bead_recv,
):
    atoms = mass_ref.shape[1]
    hid = w_feat_ref.shape[0]
    atom, bead = lax.axis_index("atom"), lax.axis_index("bead")
    rels = [r for r in range(first, first + span) if r != 0]

    def peer(rel):
        return (bead, lax.rem(atom + rel + shards, shards))

    def side(step):
        return (lax.rem(bead + step + beads, beads), atom)

    barrier = pltpu.get_barrier_semaphore()
    for rel in rels:
        pl.semaphore_signal(barrier, inc=1, device_id=peer(rel), device_id_type=MESH)
    for step in (1, -1):
        pl.semaphore_signal(barrier, inc=1, device_id=side(step), device_id_type=MESH)

    half = vel_ref[:, 0, :] + (0.5 * TIME_STEP) * force_ref[:, 0, :] / mass_ref[...]
    moved = pos_ref[:, 0, :] + TIME_STEP * half
    mine[0:3, :] = moved
    mine[3:8, :] = jnp.zeros((5, atoms), f32)
    pl.semaphore_wait(barrier, len(rels) + 2)

    bead_copies = []
    for k, step in enumerate((1, -1)):
        copy = pltpu.make_async_remote_copy(
            src_ref=mine, dst_ref=sides.at[k], send_sem=bead_send.at[k],
            recv_sem=bead_recv.at[k], device_id=side(step), device_id_type=MESH,
        )
        copy.start()
        bead_copies.append(copy)

    hot = one_hot_slots(slots_ref, atom, atoms).astype(bf16)
    projected = dot(w_feat_ref[...], feat_ref[0]).astype(bf16)
    sorted_proj = dot(projected, hot).astype(bf16)
    parts = jnp.concatenate([p.astype(f32) for p in split3(moved)] + [jnp.zeros((7, atoms), f32)], axis=0)
    sorted_pos = dot(parts.astype(bf16), hot).astype(bf16)
    own = -first
    rim_ref[own, 0:hid, :] = sorted_proj
    rim_ref[own, hid : hid + 16, :] = sorted_pos
    copies = []
    for rel in rels:
        slot = rel - first
        copy = pltpu.make_async_remote_copy(
            src_ref=rim_ref.at[own], dst_ref=rim_ref.at[slot], send_sem=send_sems.at[slot],
            recv_sem=recv_sems.at[slot], device_id=peer(-rel), device_id_type=MESH,
        )
        copy.start()
        copies.append(copy)
    for copy in bead_copies:
        copy.wait()
    spring = -OMEGA_SQ * mass_ref[...] * (2.0 * moved - sides[0, 0:3, :] - sides[1, 0:3, :])
    state_ref[0] = moved
    state_ref[1] = half
    state_ref[2] = spring
    for copy in copies:
        copy.wait()


def lanes_of(table, index):
    return jnp.take_along_axis(table, index, axis=1, mode="promise_in_bounds")


def column_of(row):
    n = row.shape[1]
    eye = iota((n, n), 0) == iota((n, n), 1)
    return jnp.sum(jnp.where(eye, row, 0.0), axis=1, keepdims=True)


def wrapped(c, box):
    return c - box * jnp.floor(c / box + 0.5)


def pair_kernel(
    shards, span, first, named,
    tiles_ref, rim_ref, state_ref, mass_ref, slots_ref, wb_ref, bias_ref, wo_ref,
    pos_out, vel_out, force_out,
    pos_all, proj_all, spread, fwd, bwd, wo_col, row_terms, packed, acc, dist_ref, energy_ref, slope_ref, pair_ref,
):
    atoms = mass_ref.shape[1]
    hid, nb = wb_ref.shape
    here = atoms // TILE
    blocks_all = here * shards
    boxes = (SIDE_LENGTH, SIDE_LENGTH, blocks_all * LAYER_WIDTH)
    atom = lax.axis_index("atom")
    own = -first * here
    up_rows, dn_rows = STACK * hid, STACK * nb

    take_h = jnp.where(lax.rem(iota((up_rows, hid), 0), hid) == iota((up_rows, hid), 1), 1.0, 0.0)
    take_j = jnp.where(lax.rem(iota((dn_rows, nb), 0), nb) == iota((dn_rows, nb), 1), 1.0, 0.0)
    wb = wb_ref[...]
    tall = dot(take_h.astype(bf16), wb).astype(bf16)
    wide = dot(tall, take_j.astype(bf16), ((1,), (1,)))
    fwd[...] = jnp.where(
        iota((up_rows, dn_rows), 0) // hid == iota((up_rows, dn_rows), 1) // nb, wide, 0.0
    ).astype(bf16)
    back = dot(take_j.astype(bf16), tall, ((1,), (1,)))
    bwd[...] = jnp.where(
        iota((dn_rows, up_rows), 0) // nb == iota((dn_rows, up_rows), 1) // hid, back, 0.0
    ).astype(bf16)
    wo_col[...] = jnp.broadcast_to(
        jnp.sum(take_h * wo_ref[...], axis=1, keepdims=True), wo_col.shape
    )
    bias = column_of(bias_ref[...])
    centres = CUTOFF * (lax.rem(iota((dn_rows, TILE), 0), nb).astype(f32) + 0.5) / nb
    for c in range(span):
        parts = rim_ref[c, hid : hid + 16, :].astype(f32)
        whole = parts[0:3] + (parts[3:6] + parts[6:9])
        proj = rim_ref[c, 0:hid, :].astype(f32)
        for b in range(here):
            pos_all[c * here + b, 0:3, :] = whole[:, b * TILE : (b + 1) * TILE]
            proj_all[c * here + b] = proj[:, b * TILE : (b + 1) * TILE]
    before = jnp.where(iota((TILE, TILE), 0) < iota((TILE, TILE), 1), 1.0, 0.0).astype(bf16)
    lane = iota((TILE, TILE), 1)
    row = iota((TILE, TILE), 0)
    row_of = SLOT * 0 + LROWS * (iota((LROWS, TILE), 1) // SLOT) + iota((LROWS, TILE), 0)

    def one_block(blk, _):
        mine = own + blk
        rows_pos = pos_all[mine]
        rows_col = [column_of(rows_pos[d : d + 1]) for d in range(3)]
        for d in range(3):
            spread[d] = lanes_of(jnp.broadcast_to(rows_pos[d : d + 1], (LROWS, TILE)), row_of)
        rows_proj = proj_all[mine] + bias
        for q in range(LROWS):
            row_terms[q] = lanes_of(rows_proj, jnp.broadcast_to(row_of[q : q + 1], (hid, TILE)))
        acc[...] = jnp.zeros_like(acc)

        def one_tile(l, _):
            block_id = lax.rem((atom + first) * here + l + blocks_all * 2, blocks_all)
            count = jnp.int32(0)
            for k in range(named):
                count += jnp.where(tiles_ref[blk, k] == block_id, 1, 0).astype(i32)

            @pl.when(count > 0)
            def _():
                cols_pos = pos_all[l]
                dist_sq = jnp.zeros((TILE, TILE), f32)
                for d in range(3):
                    c = cols_pos[d : d + 1] - rows_col[d]
                    c = c - boxes[d] * jnp.floor(c * (1.0 / boxes[d]) + 0.5)
                    dist_sq += c * c
                near = (dist_sq < CUTOFF * CUTOFF + 1e-3) & ((row != lane) | (l != mine))
                marks = jnp.where(near, 1.0, 0.0)
                ahead = dot(marks.astype(bf16), before)
                most = jnp.max(jnp.sum(marks, axis=1, keepdims=True)).astype(i32)
                move = lane - ahead.astype(i32)
                x = jnp.where(near, move * 256 + lane + 128, 0)
                step = 1
                while step < TILE:
                    bit = step * 256
                    come = pltpu.roll(x, TILE - step, 1)
                    x = jnp.where((come & bit) != 0, come, jnp.where((x & bit) != 0, 0, x))
                    step *= 2
                packed[...] = x & 255

                def one_pass(turn, _):
                    parts = []
                    for i in range(SEGS):
                        part = packed[i * LROWS : (i + 1) * LROWS, :]
                        parts.append(pltpu.roll(part, lax.rem(i * SLOT - turn * SLOT + TILE, TILE), 1))
                    seg = iota((LROWS, TILE), 1) // SLOT
                    code = parts[0]
                    for i in range(1, SEGS):
                        code = jnp.where(seg == i, parts[i], code)
                    live = code >= 128
                    index = code & 127
                    disp = []
                    dist_sq = None
                    for d in range(3):
                        c = lanes_of(jnp.broadcast_to(cols_pos[d : d + 1], (LROWS, TILE)), index)
                        c = wrapped(c - spread[d], boxes[d])
                        disp.append(c)
                        dist_sq = c * c if dist_sq is None else dist_sq + c * c
                    distance = jnp.sqrt(dist_sq + SOFTEN)
                    dist_ref[...] = distance
                    pair_ref[...] = index
                    cols_proj = proj_all[l]
                    for half in range(LROWS // (2 * STACK)):
                        offs, vals, terms = [], [], []
                        for g in range(2):
                            base = (2 * half + g) * STACK
                            off = jnp.concatenate(
                                [
                                    jnp.broadcast_to(dist_ref[base + r : base + r + 1, :], (nb, TILE))
                                    for r in range(STACK)
                                ],
                                axis=0,
                            ) - centres
                            offs.append(off)
                            vals.append(jnp.exp(-BASIS_SHARPNESS * off * off))
                            terms.append(
                                jnp.concatenate(
                                    [
                                        row_terms[base + r]
                                        + lanes_of(
                                            cols_proj,
                                            jnp.broadcast_to(pair_ref[base + r : base + r + 1, :], (hid, TILE)),
                                        )
                                        for r in range(STACK)
                                    ],
                                    axis=0,
                                )
                            )
                        basis = jnp.concatenate([v.astype(bf16) for v in vals], axis=1)
                        pre = dot(fwd[...], basis)
                        backs = []
                        for g in range(2):
                            base = (2 * half + g) * STACK
                            act = jnp.tanh(pre[:, g * TILE : (g + 1) * TILE] + terms[g])
                            wo = wo_col[...]
                            en = wo * act
                            for r in range(STACK):
                                energy_ref[base + r : base + r + 1, :] = jnp.sum(
                                    en[r * hid : (r + 1) * hid], axis=0, keepdims=True
                                )
                            backs.append((wo * (1.0 - act * act)).astype(bf16))
                        grad = dot(bwd[...], jnp.concatenate(backs, axis=1))
                        for g in range(2):
                            base = (2 * half + g) * STACK
                            part = grad[:, g * TILE : (g + 1) * TILE] * (offs[g] * vals[g])
                            for r in range(STACK):
                                slope_ref[base + r : base + r + 1, :] = jnp.sum(
                                    part[r * nb : (r + 1) * nb], axis=0, keepdims=True
                                )
                    inner = jnp.maximum(1.0 - dist_sq / (CUTOFF * CUTOFF), 0.0)
                    de_ds = (-2.0 * inner / (CUTOFF * CUTOFF)) * energy_ref[...] + inner * inner * (
                        -BASIS_SHARPNESS * slope_ref[...] / distance
                    )
                    scale = jnp.where(live, de_ds, 0.0) * (2.0 * count.astype(f32))
                    for d in range(3):
                        acc[d] += scale * disp[d]
                    return 0

                lax.fori_loop(0, (most + SLOT - 1) // SLOT, one_pass, 0)

            return 0

        lax.fori_loop(0, span * here, one_tile, 0)
        seg_sum = jnp.where(row // SLOT == lane // LROWS, 1.0, 0.0)
        mineq = lax.rem(iota((LROWS, TILE), 1), LROWS) == iota((LROWS, TILE), 0)
        for d in range(3):
            s = dot(acc[d], seg_sum, exact=True)
            pos_all[span * here + blk, d : d + 1, :] = jnp.sum(jnp.where(mineq, s, 0.0), axis=0, keepdims=True)
        return 0

    pos_all[span * here :] = jnp.zeros((here, 8, TILE), f32)
    lax.fori_loop(0, here, one_block, 0)
    by_slot = jnp.concatenate([pos_all[span * here + b] for b in range(here)], axis=1)
    hot = one_hot_slots(slots_ref, atom, atoms)
    pair = dot(by_slot, hot, ((1,), (1,)), exact=True)[0:3]
    moved, half, spring = state_ref[0], state_ref[1], state_ref[2]
    force = pair + spring
    pos_out[:, 0, :] = moved
    force_out[:, 0, :] = force
    vel_out[:, 0, :] = half + (0.5 * TIME_STEP) * force / mass_ref[...]


def body(
    positions, velocities, forces_now, masses, features, tile_blocks, block_slots,
    w_basis, w_feat, hidden_bias, w_out,
):
    atoms = positions.shape[2]
    hid, nb = w_basis.shape
    here = atoms // TILE
    shards, beads = lax.axis_size("atom"), lax.axis_size("bead")
    span, first = window(here, shards)
    mass_row = masses.reshape(1, atoms)
    slot_row = block_slots.reshape(1, atoms)
    vmem = pl.BlockSpec(memory_space=pltpu.VMEM)
    rim, state = pl.pallas_call(
        functools.partial(exchange_kernel, shards, beads, span, first),
        out_shape=(
            jax.ShapeDtypeStruct((span, hid + 16, atoms), bf16),
            jax.ShapeDtypeStruct((3, 3, atoms), f32),
        ),
        in_specs=[vmem] * 7,
        out_specs=(vmem, vmem),
        scratch_shapes=[
            pltpu.VMEM((8, atoms), f32),
            pltpu.VMEM((2, 8, atoms), f32),
            pltpu.SemaphoreType.DMA((span,)),
            pltpu.SemaphoreType.DMA((span,)),
            pltpu.SemaphoreType.DMA((2,)),
            pltpu.SemaphoreType.DMA((2,)),
        ],
        compiler_params=pltpu.CompilerParams(collective_id=0, has_side_effects=True),
        name="exchange",
    )(positions, velocities, forces_now, mass_row, features, slot_row, w_feat)
    out = jax.ShapeDtypeStruct(positions.shape, f32)
    return pl.pallas_call(
        functools.partial(pair_kernel, shards, span, first, tile_blocks.shape[1]),
        out_shape=(out, out, out),
        in_specs=[pl.BlockSpec(memory_space=pltpu.SMEM)] + [vmem] * 7,
        out_specs=(vmem, vmem, vmem),
        scratch_shapes=[
            pltpu.VMEM(((span + 1) * here, 8, TILE), f32),
            pltpu.VMEM((span * here, hid, TILE), f32),
            pltpu.VMEM((3, LROWS, TILE), f32),
            pltpu.VMEM((STACK * hid, STACK * nb), bf16),
            pltpu.VMEM((STACK * nb, STACK * hid), bf16),
            pltpu.VMEM((STACK * hid, TILE), f32),
            pltpu.VMEM((LROWS, hid, TILE), f32),
            pltpu.VMEM((TILE, TILE), i32),
            pltpu.VMEM((3, LROWS, TILE), f32),
            pltpu.VMEM((LROWS, TILE), f32),
            pltpu.VMEM((LROWS, TILE), f32),
            pltpu.VMEM((LROWS, TILE), f32),
            pltpu.VMEM((LROWS, TILE), i32),
        ],
        compiler_params=pltpu.CompilerParams(vmem_limit_bytes=32 * 1024 * 1024),
        name="pairs",
    )(
        tile_blocks, rim, state, mass_row, slot_row, w_basis,
        hidden_bias.reshape(1, hid), w_out.reshape(1, hid),
    )


def solution(mesh):
    vec = P(None, "bead", "atom")
    return jax.shard_map(
        body,
        mesh=mesh,
        in_specs=(
            vec, vec, vec, P("atom"), P("bead", None, "atom"), P("atom", None), P("atom"),
            P(), P(), P(), P(),
        ),
        out_specs=(vec, vec, vec),
        check_vma=False,
    )
```

```python
import functools

import jax
import jax.numpy as jnp
from jax import lax
from jax.experimental import pallas as pl
from jax.experimental.pallas import tpu as pltpu
from jax.sharding import PartitionSpec as P

TILE = 128
LAYER_WIDTH = 0.15
SIDE_LENGTH = 2.9
CUTOFF = 0.6
BASIS_SHARPNESS = 355.0
SOFTEN = 0.0001
TIME_STEP = 0.1
OMEGA_SQ = 100.0
REACH_BLOCKS = 4
SLOT = 16
SEGS = TILE // SLOT
LROWS = TILE // SEGS
STACK = 4
MESH = pl.DeviceIdType.MESH
f32, bf16, i32 = jnp.float32, jnp.bfloat16, jnp.int32


def iota(shape, dim):
    return lax.broadcasted_iota(i32, shape, dim)


def dot(a, b, dims=((1,), (0,)), exact=False):
    return lax.dot_general(
        a,
        b,
        (dims, ((), ())),
        precision=lax.Precision.HIGHEST if exact else None,
        preferred_element_type=f32,
    )


def split3(x):
    hi = x.astype(bf16)
    rest = x - hi.astype(f32)
    mid = rest.astype(bf16)
    low = (rest - mid.astype(f32)).astype(bf16)
    return hi, mid, low


def window(blocks_here, shards):
    reach = (REACH_BLOCKS + blocks_here - 1) // blocks_here
    span = min(2 * reach + 1, shards)
    return span, -(span // 2)


def one_hot_slots(slots_ref, shard, atoms):
    local = slots_ref[...] - shard * atoms
    return jnp.where(iota((atoms, atoms), 0) == local, 1.0, 0.0)


def exchange_kernel(
    shards, beads, span, first,
    pos_ref, vel_ref, force_ref, mass_ref, feat_ref, slots_ref, w_feat_ref, wb_ref, wo_ref,
    rim_ref, state_ref, fwd, bwd, read,
    mine, sides, send_sems, recv_sems, bead_send, bead_recv,
):
    atoms = mass_ref.shape[1]
    hid = w_feat_ref.shape[0]
    atom, bead = lax.axis_index("atom"), lax.axis_index("bead")
    rels = [r for r in range(first, first + span) if r != 0]

    def peer(rel):
        return (bead, lax.rem(atom + rel + shards, shards))

    def side(step):
        return (lax.rem(bead + step + beads, beads), atom)

    barrier = pltpu.get_barrier_semaphore()
    for rel in rels:
        pl.semaphore_signal(barrier, inc=1, device_id=peer(rel), device_id_type=MESH)
    for step in (1, -1):
        pl.semaphore_signal(barrier, inc=1, device_id=side(step), device_id_type=MESH)

    half = vel_ref[:, 0, :] + (0.5 * TIME_STEP) * force_ref[:, 0, :] / mass_ref[...]
    moved = pos_ref[:, 0, :] + TIME_STEP * half
    mine[0:3, :] = moved
    mine[3:8, :] = jnp.zeros((5, atoms), f32)
    hot = one_hot_slots(slots_ref, atom, atoms).astype(bf16)
    projected = dot(w_feat_ref[...], feat_ref[0]).astype(bf16)
    sorted_proj = dot(projected, hot).astype(bf16)
    parts = jnp.concatenate([p.astype(f32) for p in split3(moved)] + [jnp.zeros((7, atoms), f32)], axis=0)
    sorted_pos = dot(parts.astype(bf16), hot).astype(bf16)
    own = -first
    rim_ref[own, 0:hid, :] = sorted_proj
    rim_ref[own, hid : hid + 16, :] = sorted_pos
    pl.semaphore_wait(barrier, len(rels) + 2)

    bead_copies = []
    for k, step in enumerate((1, -1)):
        copy = pltpu.make_async_remote_copy(
            src_ref=mine, dst_ref=sides.at[k], send_sem=bead_send.at[k],
            recv_sem=bead_recv.at[k], device_id=side(step), device_id_type=MESH,
        )
        copy.start()
        bead_copies.append(copy)

    copies = []
    for rel in rels:
        slot = rel - first
        copy = pltpu.make_async_remote_copy(
            src_ref=rim_ref.at[own], dst_ref=rim_ref.at[slot], send_sem=send_sems.at[slot],
            recv_sem=recv_sems.at[slot], device_id=peer(-rel), device_id_type=MESH,
        )
        copy.start()
        copies.append(copy)
    nb = wb_ref.shape[0]
    up, dn = STACK * hid, STACK * nb
    take_h = jnp.where(lax.rem(iota((up, hid), 0), hid) == iota((up, hid), 1), 1.0, 0.0)
    take_j = jnp.where(lax.rem(iota((dn, nb), 0), nb) == iota((dn, nb), 1), 1.0, 0.0).astype(bf16)
    wb = wb_ref[...]
    wide = dot(dot(take_h.astype(bf16), wb, ((1,), (1,))).astype(bf16), take_j, ((1,), (1,)))
    fwd[...] = jnp.where(iota((up, dn), 0) // hid == iota((up, dn), 1) // nb, wide, 0.0).astype(bf16)
    scaled = (wb.astype(f32) * wo_ref[...]).astype(bf16)
    back = dot(dot(take_j, scaled).astype(bf16), take_h.astype(bf16), ((1,), (1,)))
    bwd[...] = jnp.where(iota((dn, up), 0) // nb == iota((dn, up), 1) // hid, back, 0.0).astype(bf16)
    wo_all = jnp.broadcast_to(wo_ref[...].astype(bf16), (16, hid))
    outs = dot(wo_all, take_h.astype(bf16), ((1,), (1,)))
    read[...] = jnp.where(iota((16, up), 0) == iota((16, up), 1) // hid, outs, 0.0).astype(bf16)
    for copy in bead_copies:
        copy.wait()
    spring = -OMEGA_SQ * mass_ref[...] * (2.0 * moved - sides[0, 0:3, :] - sides[1, 0:3, :])
    state_ref[0] = moved
    state_ref[1] = half
    state_ref[2] = spring
    for copy in copies:
        copy.wait()


def lanes_of(table, index):
    return jnp.take_along_axis(table, index, axis=1, mode="promise_in_bounds")


def column_of(row):
    n = row.shape[1]
    eye = iota((n, n), 0) == iota((n, n), 1)
    return jnp.sum(jnp.where(eye, row, 0.0), axis=1, keepdims=True)


def wrapped(c, box):
    return c - box * jnp.floor(c / box + 0.5)


def pair_kernel(
    shards, span, first, named,
    tiles_ref, rim_ref, state_ref, mass_ref, slots_ref, fwd, bwd, read, bias_ref,
    pos_out, vel_out, force_out,
    pos_all, proj_all, spread, row_cols, row_terms, packed, acc, sums, dist_ref, pair_ref, energy_ref, slope_ref,
    entry_count, entry_blk, entry_tile, jobs,
):
    atoms = mass_ref.shape[1]
    hid = bias_ref.shape[1]
    nb = bwd.shape[0] // STACK
    here = atoms // TILE
    blocks_all = here * shards
    boxes = (SIDE_LENGTH, SIDE_LENGTH, blocks_all * LAYER_WIDTH)
    atom = lax.axis_index("atom")
    own = -first * here

    bias = column_of(bias_ref[...])
    centres = CUTOFF * (lax.rem(iota((STACK * nb, TILE), 0), nb).astype(f32) + 0.5) / nb
    for c in range(span):
        parts = rim_ref[c, hid : hid + 16, :].astype(f32)
        whole = parts[0:3] + (parts[3:6] + parts[6:9])
        proj = rim_ref[c, 0:hid, :].astype(f32)
        for b in range(here):
            pos_all[c * here + b, 0:3, :] = whole[:, b * TILE : (b + 1) * TILE]
            proj_all[c * here + b] = proj[:, b * TILE : (b + 1) * TILE]
    before = jnp.where(iota((TILE, TILE), 0) < iota((TILE, TILE), 1), 1.0, 0.0).astype(bf16)
    lane = iota((TILE, TILE), 1)
    row = iota((TILE, TILE), 0)
    seg = iota((LROWS, TILE), 1) // SLOT
    row_of = LROWS * seg + iota((LROWS, TILE), 0)

    for blk in range(here):
        rows_pos = pos_all[own + blk]
        for d in range(3):
            row_cols[blk * 3 + d] = jnp.broadcast_to(column_of(rows_pos[d : d + 1]), (TILE, TILE))
            spread[blk * 3 + d] = lanes_of(jnp.broadcast_to(rows_pos[d : d + 1], (LROWS, TILE)), row_of)
        rows_proj = proj_all[own + blk] + bias
        for q in range(LROWS):
            row_terms[blk * LROWS + q] = lanes_of(rows_proj, jnp.broadcast_to(row_of[q : q + 1], (hid, TILE)))
    acc[...] = jnp.zeros_like(acc)

    def list_entry(at, n):
        blk, l = at // (span * here), lax.rem(at, span * here)
        block_id = lax.rem((atom + first) * here + l + blocks_all * 2, blocks_all)
        count = jnp.int32(0)
        for k in range(named):
            count += jnp.where(tiles_ref[blk, k] == block_id, 1, 0).astype(i32)
        entry_count[n] = count
        entry_blk[n] = blk
        entry_tile[n] = l
        return n + jnp.where(count > 0, 1, 0).astype(i32)

    entries = lax.fori_loop(0, here * span * here, list_entry, jnp.int32(0))
    entry_count[entries] = 0
    entry_blk[entries] = 0
    entry_tile[entries] = 0
    packed[entries] = jnp.zeros((TILE, TILE), i32)

    def compact(e):
        blk, l = entry_blk[e], entry_tile[e]
        cols_pos = pos_all[l]
        dist_sq = None
        for d in range(3):
            c = cols_pos[d : d + 1] - row_cols[blk * 3 + d]
            c = c - boxes[d] * jnp.floor(c * (1.0 / boxes[d]) + 0.5)
            dist_sq = c * c if dist_sq is None else dist_sq + c * c
        limit = jnp.where(entry_count[e] > 0, CUTOFF * CUTOFF + 1e-3, -1.0).astype(f32)
        near = (dist_sq < limit) & (row - lane != jnp.where(l == own + blk, 0, 2 * TILE))
        marks = jnp.where(near, 1.0, 0.0)
        ahead = dot(marks.astype(bf16), before)
        most = jnp.max(ahead[:, TILE - 1 :] + marks[:, TILE - 1 :]).astype(i32)
        x = jnp.where(near, (lane - ahead.astype(i32)) * 256 + lane + 128, 0)
        step = 1
        while step < TILE:
            bit = step * 256
            come = pltpu.roll(x, TILE - step, 1)
            x = jnp.where((come & bit) != 0, come, jnp.where((x & bit) != 0, 0, x))
            step *= 2
        packed[e] = x & 255
        return most

    def list_jobs(it, n):
        mosts = [compact(2 * it + u) for u in range(2)]
        for u in range(2):
            turns = (mosts[u] + SLOT - 1) // SLOT

            def add(turn, _, u=u, n=n):
                jobs[n + turn] = (2 * it + u) * SEGS + turn
                return 0

            lax.fori_loop(0, turns, add, 0)
            n = n + turns
        return n

    total = lax.fori_loop(0, (entries + 1) // 2, list_jobs, jnp.int32(0))
    jobs[total] = entries * SEGS

    def one_job(u, job):
        e, turn = job // SEGS, lax.rem(job, SEGS)
        blk, l = entry_blk[e], entry_tile[e]
        code = None
        for i in range(SEGS):
            part = packed[e, i * LROWS : (i + 1) * LROWS, :]
            part = pltpu.roll(part, lax.rem((i - turn) * SLOT + TILE, TILE), 1)
            code = part if code is None else jnp.where(seg == i, part, code)
        live = code >= 128
        index = code & 127
        disp = []
        dist_sq = None
        for d in range(3):
            c = lanes_of(jnp.broadcast_to(pos_all[l, d : d + 1, :], (LROWS, TILE)), index)
            c = wrapped(c - spread[blk * 3 + d], boxes[d])
            disp.append(c)
            dist_sq = c * c if dist_sq is None else dist_sq + c * c
        distance = jnp.sqrt(dist_sq + SOFTEN)
        dist_ref[u] = distance
        pair_ref[u] = index
        cols_proj = proj_all[l]
        for half in range(LROWS // (2 * STACK)):
            offs, vals, terms = [], [], []
            for g in range(2):
                base = (2 * half + g) * STACK
                rows = range(base, base + STACK)
                off = jnp.concatenate(
                    [jnp.broadcast_to(dist_ref[u, q : q + 1, :], (nb, TILE)) for q in rows], axis=0
                ) - centres
                val = jnp.exp(-BASIS_SHARPNESS * off * off)
                vals.append(val.astype(bf16))
                offs.append(off * val)
                terms.append(
                    jnp.concatenate(
                        [
                            row_terms[blk * LROWS + q]
                            + lanes_of(cols_proj, jnp.broadcast_to(pair_ref[u, q : q + 1, :], (hid, TILE)))
                            for q in rows
                        ],
                        axis=0,
                    )
                )
            pre = dot(fwd[...], jnp.concatenate(vals, axis=1)) + jnp.concatenate(terms, axis=1)
            act = jnp.tanh(pre.astype(bf16))
            energy = dot(read[...], act)
            grad = dot(bwd[...], 1.0 - act * act)
            for g in range(2):
                base = (2 * half + g) * STACK
                part = grad[:, g * TILE : (g + 1) * TILE] * offs[g]
                energy_ref[u, base : base + STACK, :] = energy[0:STACK, g * TILE : (g + 1) * TILE]
                for r in range(STACK):
                    slope_ref[u, base + r : base + r + 1, :] = jnp.sum(
                        part[r * nb : (r + 1) * nb], axis=0, keepdims=True
                    )
        inner = jnp.maximum(1.0 - dist_sq / (CUTOFF * CUTOFF), 0.0)
        de_ds = (-2.0 * inner / (CUTOFF * CUTOFF)) * energy_ref[u] + inner * inner * (
            -BASIS_SHARPNESS * slope_ref[u] / distance
        )
        scale = jnp.where(live, de_ds, 0.0) * (2.0 * entry_count[e].astype(f32))
        return blk, [scale * c for c in disp]

    def job_pair(it, _):
        done = [one_job(u, jobs[2 * it + u]) for u in range(2)]
        for blk, forces in done:
            for d in range(3):
                acc[blk * 3 + d] += forces[d]
        return 0

    lax.fori_loop(0, (total + 1) // 2, job_pair, 0)

    seg_sum = jnp.where(row // SLOT == lane // LROWS, 1.0, 0.0)
    mine = lax.rem(iota((LROWS, TILE), 1), LROWS) == iota((LROWS, TILE), 0)
    sums[...] = jnp.zeros_like(sums)
    for blk in range(here):
        for d in range(3):
            s = dot(acc[blk * 3 + d], seg_sum, exact=True)
            sums[d : d + 1, blk * TILE : (blk + 1) * TILE] = jnp.sum(
                jnp.where(mine, s, 0.0), axis=0, keepdims=True
            )
    hot = one_hot_slots(slots_ref, atom, atoms)
    pair = dot(sums[...], hot, ((1,), (1,)), exact=True)[0:3]
    moved, half, spring = state_ref[0], state_ref[1], state_ref[2]
    force = pair + spring
    pos_out[:, 0, :] = moved
    force_out[:, 0, :] = force
    vel_out[:, 0, :] = half + (0.5 * TIME_STEP) * force / mass_ref[...]


def body(
    positions, velocities, forces_now, masses, features, tile_blocks, block_slots,
    w_basis, w_feat, hidden_bias, w_out,
):
    atoms = positions.shape[2]
    hid, nb = w_basis.shape
    here = atoms // TILE
    shards, beads = lax.axis_size("atom"), lax.axis_size("bead")
    span, first = window(here, shards)
    mass_row = masses.reshape(1, atoms)
    slot_row = block_slots.reshape(1, atoms)
    vmem = pl.BlockSpec(memory_space=pltpu.VMEM)
    rim, state, fwd, bwd, read = pl.pallas_call(
        functools.partial(exchange_kernel, shards, beads, span, first),
        out_shape=(
            jax.ShapeDtypeStruct((span, hid + 16, atoms), bf16),
            jax.ShapeDtypeStruct((3, 3, atoms), f32),
            jax.ShapeDtypeStruct((STACK * hid, STACK * nb), bf16),
            jax.ShapeDtypeStruct((STACK * nb, STACK * hid), bf16),
            jax.ShapeDtypeStruct((16, STACK * hid), bf16),
        ),
        in_specs=[vmem] * 9,
        out_specs=(vmem,) * 5,
        scratch_shapes=[
            pltpu.VMEM((8, atoms), f32),
            pltpu.VMEM((2, 8, atoms), f32),
            pltpu.SemaphoreType.DMA((span,)),
            pltpu.SemaphoreType.DMA((span,)),
            pltpu.SemaphoreType.DMA((2,)),
            pltpu.SemaphoreType.DMA((2,)),
        ],
        compiler_params=pltpu.CompilerParams(collective_id=0, has_side_effects=True),
        name="exchange",
    )(positions, velocities, forces_now, mass_row, features, slot_row, w_feat, w_basis.T, w_out.reshape(1, hid))
    out = jax.ShapeDtypeStruct(positions.shape, f32)
    entries = here * span * here + 2
    return pl.pallas_call(
        functools.partial(pair_kernel, shards, span, first, tile_blocks.shape[1]),
        out_shape=(out, out, out),
        in_specs=[pl.BlockSpec(memory_space=pltpu.SMEM)] + [vmem] * 8,
        out_specs=(vmem, vmem, vmem),
        scratch_shapes=[
            pltpu.VMEM((span * here, 8, TILE), f32),
            pltpu.VMEM((span * here, hid, TILE), f32),
            pltpu.VMEM((here * 3, LROWS, TILE), f32),
            pltpu.VMEM((here * 3, TILE, TILE), f32),
            pltpu.VMEM((here * LROWS, hid, TILE), f32),
            pltpu.VMEM((entries, TILE, TILE), i32),
            pltpu.VMEM((here * 3, LROWS, TILE), f32),
            pltpu.VMEM((8, atoms), f32),
            pltpu.VMEM((2, LROWS, TILE), f32),
            pltpu.VMEM((2, LROWS, TILE), i32),
            pltpu.VMEM((2, LROWS, TILE), f32),
            pltpu.VMEM((2, LROWS, TILE), f32),
            pltpu.SMEM((entries,), i32),
            pltpu.SMEM((entries,), i32),
            pltpu.SMEM((entries,), i32),
            pltpu.SMEM((entries * SEGS + 2,), i32),
        ],
        compiler_params=pltpu.CompilerParams(vmem_limit_bytes=32 * 1024 * 1024),
        name="pairs",
    )(
        tile_blocks, rim, state, mass_row, slot_row, fwd, bwd, read,
        hidden_bias.reshape(1, hid),
    )


def solution(mesh):
    vec = P(None, "bead", "atom")
    return jax.shard_map(
        body,
        mesh=mesh,
        in_specs=(
            vec, vec, vec, P("atom"), P("bead", None, "atom"), P("atom", None), P("atom"),
            P(), P(), P(), P(),
        ),
        out_specs=(vec, vec, vec),
        check_vma=False,
    )
```

```python
import functools

import jax
import jax.numpy as jnp
from jax import lax
from jax.experimental import pallas as pl
from jax.experimental.pallas import tpu as pltpu
from jax.sharding import PartitionSpec as P

TILE = 128
LAYER_WIDTH = 0.15
SIDE_LENGTH = 2.9
CUTOFF = 0.6
BASIS_SHARPNESS = 355.0
SOFTEN = 0.0001
TIME_STEP = 0.1
OMEGA_SQ = 100.0
REACH_BLOCKS = 4
SLOT = 16
SEGS = TILE // SLOT
LROWS = TILE // SEGS
STACK = 4
MESH = pl.DeviceIdType.MESH
f32, bf16, i32 = jnp.float32, jnp.bfloat16, jnp.int32


def iota(shape, dim):
    return lax.broadcasted_iota(i32, shape, dim)


def dot(a, b, dims=((1,), (0,)), exact=False):
    return lax.dot_general(
        a,
        b,
        (dims, ((), ())),
        precision=lax.Precision.HIGHEST if exact else None,
        preferred_element_type=f32,
    )


def split3(x):
    hi = x.astype(bf16)
    rest = x - hi.astype(f32)
    mid = rest.astype(bf16)
    low = (rest - mid.astype(f32)).astype(bf16)
    return hi, mid, low


def window(blocks_here, shards):
    reach = (REACH_BLOCKS + blocks_here - 1) // blocks_here
    span = min(2 * reach + 1, shards)
    return span, -(span // 2)


def one_hot_slots(slots_ref, shard, atoms):
    local = slots_ref[...] - shard * atoms
    return jnp.where(iota((atoms, atoms), 0) == local, 1.0, 0.0)


def exchange_kernel(
    shards, beads, span, first,
    pos_ref, vel_ref, force_ref, mass_ref, feat_ref, slots_ref, w_feat_ref, wb_ref, wo_ref,
    rim_ref, state_ref, fwd, bwd, read,
    mine, sides, send_sems, recv_sems, bead_send, bead_recv,
):
    atoms = mass_ref.shape[1]
    hid = w_feat_ref.shape[0]
    atom, bead = lax.axis_index("atom"), lax.axis_index("bead")
    rels = [r for r in range(first, first + span) if r != 0]

    def peer(rel):
        return (bead, lax.rem(atom + rel + shards, shards))

    def side(step):
        return (lax.rem(bead + step + beads, beads), atom)

    barrier = pltpu.get_barrier_semaphore()
    for rel in rels:
        pl.semaphore_signal(barrier, inc=1, device_id=peer(rel), device_id_type=MESH)
    for step in (1, -1):
        pl.semaphore_signal(barrier, inc=1, device_id=side(step), device_id_type=MESH)

    half = vel_ref[:, 0, :] + (0.5 * TIME_STEP) * force_ref[:, 0, :] / mass_ref[...]
    moved = pos_ref[:, 0, :] + TIME_STEP * half
    mine[0:3, :] = moved
    mine[3:8, :] = jnp.zeros((5, atoms), f32)
    hot = one_hot_slots(slots_ref, atom, atoms).astype(bf16)
    projected = dot(w_feat_ref[...], feat_ref[0]).astype(bf16)
    sorted_proj = dot(projected, hot).astype(bf16)
    parts = jnp.concatenate([p.astype(f32) for p in split3(moved)] + [jnp.zeros((7, atoms), f32)], axis=0)
    sorted_pos = dot(parts.astype(bf16), hot).astype(bf16)
    own = -first
    rim_ref[own, 0:hid, :] = sorted_proj
    rim_ref[own, hid : hid + 16, :] = sorted_pos
    pl.semaphore_wait(barrier, len(rels) + 2)

    bead_copies = []
    for k, step in enumerate((1, -1)):
        copy = pltpu.make_async_remote_copy(
            src_ref=mine, dst_ref=sides.at[k], send_sem=bead_send.at[k],
            recv_sem=bead_recv.at[k], device_id=side(step), device_id_type=MESH,
        )
        copy.start()
        bead_copies.append(copy)

    copies = []
    for rel in rels:
        slot = rel - first
        copy = pltpu.make_async_remote_copy(
            src_ref=rim_ref.at[own], dst_ref=rim_ref.at[slot], send_sem=send_sems.at[slot],
            recv_sem=recv_sems.at[slot], device_id=peer(-rel), device_id_type=MESH,
        )
        copy.start()
        copies.append(copy)
    nb = wb_ref.shape[0]
    up, dn = STACK * hid, STACK * nb
    take_h = jnp.where(lax.rem(iota((up, hid), 0), hid) == iota((up, hid), 1), 1.0, 0.0)
    take_j = jnp.where(lax.rem(iota((dn, nb), 0), nb) == iota((dn, nb), 1), 1.0, 0.0).astype(bf16)
    wb = wb_ref[...]
    wide = dot(dot(take_h.astype(bf16), wb, ((1,), (1,))).astype(bf16), take_j, ((1,), (1,)))
    fwd[...] = jnp.where(iota((up, dn), 0) // hid == iota((up, dn), 1) // nb, wide, 0.0).astype(bf16)
    scaled = (wb.astype(f32) * wo_ref[...]).astype(bf16)
    back = dot(dot(take_j, scaled).astype(bf16), take_h.astype(bf16), ((1,), (1,)))
    bwd[...] = jnp.where(iota((dn, up), 0) // nb == iota((dn, up), 1) // hid, back, 0.0).astype(bf16)
    wo_all = jnp.broadcast_to(wo_ref[...].astype(bf16), (16, hid))
    outs = dot(wo_all, take_h.astype(bf16), ((1,), (1,)))
    read[...] = jnp.where(iota((16, up), 0) == iota((16, up), 1) // hid, outs, 0.0).astype(bf16)
    for copy in bead_copies:
        copy.wait()
    spring = -OMEGA_SQ * mass_ref[...] * (2.0 * moved - sides[0, 0:3, :] - sides[1, 0:3, :])
    state_ref[0] = moved
    state_ref[1] = half
    state_ref[2] = spring
    for copy in copies:
        copy.wait()


def lanes_of(table, index):
    return jnp.take_along_axis(table, index, axis=1, mode="promise_in_bounds")


def column_of(row):
    n = row.shape[1]
    eye = iota((n, n), 0) == iota((n, n), 1)
    return jnp.sum(jnp.where(eye, row, 0.0), axis=1, keepdims=True)


def wrapped(c, box):
    return c - box * jnp.floor(c / box + 0.5)


def pair_kernel(
    shards, span, first, named,
    tiles_ref, rim_ref, state_ref, mass_ref, slots_ref, fwd, bwd, read, bias_ref,
    pos_out, vel_out, force_out,
    pos_all, proj_all, spread, row_cols, row_terms, packed, acc, sums, dist_ref, pair_ref, energy_ref, slope_ref,
    entry_count, entry_blk, entry_tile, jobs,
):
    atoms = mass_ref.shape[1]
    hid = bias_ref.shape[1]
    nb = bwd.shape[0] // STACK
    here = atoms // TILE
    blocks_all = here * shards
    boxes = (SIDE_LENGTH, SIDE_LENGTH, blocks_all * LAYER_WIDTH)
    atom = lax.axis_index("atom")
    own = -first * here

    bias = column_of(bias_ref[...])
    centres = CUTOFF * (lax.rem(iota((STACK * nb, TILE), 0), nb).astype(f32) + 0.5) / nb
    for c in range(span):
        parts = rim_ref[c, hid : hid + 16, :].astype(f32)
        whole = parts[0:3] + (parts[3:6] + parts[6:9])
        proj = rim_ref[c, 0:hid, :].astype(f32)
        for b in range(here):
            pos_all[c * here + b, 0:3, :] = whole[:, b * TILE : (b + 1) * TILE]
            proj_all[c * here + b] = proj[:, b * TILE : (b + 1) * TILE]
    before = jnp.where(iota((TILE, TILE), 0) < iota((TILE, TILE), 1), 1.0, 0.0).astype(bf16)
    lane = iota((TILE, TILE), 1)
    row = iota((TILE, TILE), 0)
    seg = iota((LROWS, TILE), 1) // SLOT
    row_of = LROWS * seg + iota((LROWS, TILE), 0)

    for blk in range(here):
        rows_pos = pos_all[own + blk]
        for d in range(3):
            row_cols[blk * 3 + d] = jnp.broadcast_to(column_of(rows_pos[d : d + 1]), (TILE, TILE))
            spread[blk * 3 + d] = lanes_of(jnp.broadcast_to(rows_pos[d : d + 1], (LROWS, TILE)), row_of)
        rows_proj = proj_all[own + blk] + bias
        for q in range(LROWS):
            row_terms[blk * LROWS + q] = lanes_of(rows_proj, jnp.broadcast_to(row_of[q : q + 1], (hid, TILE)))
    acc[...] = jnp.zeros_like(acc)

    def list_entry(at, n):
        blk, l = at // (span * here), lax.rem(at, span * here)
        block_id = lax.rem((atom + first) * here + l + blocks_all * 2, blocks_all)
        count = jnp.int32(0)
        for k in range(named):
            count += jnp.where(tiles_ref[blk, k] == block_id, 1, 0).astype(i32)
        entry_count[n] = count
        entry_blk[n] = blk
        entry_tile[n] = l
        return n + jnp.where(count > 0, 1, 0).astype(i32)

    entries = lax.fori_loop(0, here * span * here, list_entry, jnp.int32(0))
    entry_count[entries] = 0
    entry_blk[entries] = 0
    entry_tile[entries] = 0
    packed[entries] = jnp.zeros((TILE, TILE), i32)

    def compact(e):
        blk, l = entry_blk[e], entry_tile[e]
        cols_pos = pos_all[l]
        dist_sq = None
        for d in range(3):
            c = cols_pos[d : d + 1] - row_cols[blk * 3 + d]
            c = c - boxes[d] * jnp.floor(c * (1.0 / boxes[d]) + 0.5)
            dist_sq = c * c if dist_sq is None else dist_sq + c * c
        limit = jnp.where(entry_count[e] > 0, CUTOFF * CUTOFF + 1e-3, -1.0).astype(f32)
        near = (dist_sq < limit) & (row - lane != jnp.where(l == own + blk, 0, 2 * TILE))
        marks = jnp.where(near, 1.0, 0.0)
        ahead = dot(marks.astype(bf16), before)
        most = jnp.max(ahead[:, TILE - 1 :] + marks[:, TILE - 1 :]).astype(i32)
        x = jnp.where(near, (lane - ahead.astype(i32)) * 256 + lane + 128, 0)
        step = 1
        while step < TILE:
            bit = step * 256
            come = pltpu.roll(x, TILE - step, 1)
            x = jnp.where((come & bit) != 0, come, jnp.where((x & bit) != 0, 0, x))
            step *= 2
        packed[e] = x & 255
        return most

    def list_jobs(it, n):
        mosts = [compact(2 * it + u) for u in range(2)]
        for u in range(2):
            turns = (mosts[u] + SLOT - 1) // SLOT

            def add(turn, _, u=u, n=n):
                jobs[n + turn] = (2 * it + u) * SEGS + turn
                return 0

            lax.fori_loop(0, turns, add, 0)
            n = n + turns
        return n

    total = lax.fori_loop(0, (entries + 1) // 2, list_jobs, jnp.int32(0))
    jobs[total] = entries * SEGS

    def one_job(u, job):
        e, turn = job // SEGS, lax.rem(job, SEGS)
        blk, l = entry_blk[e], entry_tile[e]
        code = None
        for i in range(SEGS):
            part = packed[e, i * LROWS : (i + 1) * LROWS, :]
            part = pltpu.roll(part, lax.rem((i - turn) * SLOT + TILE, TILE), 1)
            code = part if code is None else jnp.where(seg == i, part, code)
        live = code >= 128
        index = code & 127
        disp = []
        dist_sq = None
        for d in range(3):
            c = lanes_of(jnp.broadcast_to(pos_all[l, d : d + 1, :], (LROWS, TILE)), index)
            c = wrapped(c - spread[blk * 3 + d], boxes[d])
            disp.append(c)
            dist_sq = c * c if dist_sq is None else dist_sq + c * c
        distance = jnp.sqrt(dist_sq + SOFTEN)
        dist_ref[u] = distance
        pair_ref[u] = index
        cols_proj = proj_all[l]
        for half in range(LROWS // (2 * STACK)):
            offs, vals, terms = [], [], []
            for g in range(2):
                base = (2 * half + g) * STACK
                rows = range(base, base + STACK)
                off = jnp.concatenate(
                    [jnp.broadcast_to(dist_ref[u, q : q + 1, :], (nb, TILE)) for q in rows], axis=0
                ) - centres
                val = jnp.exp(-BASIS_SHARPNESS * off * off)
                vals.append(val.astype(bf16))
                offs.append(off * val)
                terms.append(
                    jnp.concatenate(
                        [
                            row_terms[blk * LROWS + q]
                            + lanes_of(cols_proj, jnp.broadcast_to(pair_ref[u, q : q + 1, :], (hid, TILE)))
                            for q in rows
                        ],
                        axis=0,
                    )
                )
            pre = dot(fwd[...], jnp.concatenate(vals, axis=1)) + jnp.concatenate(terms, axis=1)
            act = jnp.tanh(pre.astype(bf16))
            energy = dot(read[...], act)
            grad = dot(bwd[...], 1.0 - act * act)
            for g in range(2):
                base = (2 * half + g) * STACK
                part = grad[:, g * TILE : (g + 1) * TILE] * offs[g]
                energy_ref[u, base : base + STACK, :] = energy[0:STACK, g * TILE : (g + 1) * TILE]
                for r in range(STACK):
                    slope_ref[u, base + r : base + r + 1, :] = jnp.sum(
                        part[r * nb : (r + 1) * nb], axis=0, keepdims=True
                    )
        inner = jnp.maximum(1.0 - dist_sq / (CUTOFF * CUTOFF), 0.0)
        de_ds = (-2.0 * inner / (CUTOFF * CUTOFF)) * energy_ref[u] + inner * inner * (
            -BASIS_SHARPNESS * slope_ref[u] / distance
        )
        scale = jnp.where(live, de_ds, 0.0) * (2.0 * entry_count[e].astype(f32))
        return blk, [scale * c for c in disp]

    def job_pair(it, _):
        done = [one_job(u, jobs[2 * it + u]) for u in range(2)]
        for blk, forces in done:
            for d in range(3):
                acc[blk * 3 + d] += forces[d]
        return 0

    lax.fori_loop(0, (total + 1) // 2, job_pair, 0)

    seg_sum = jnp.where(row // SLOT == lane // LROWS, 1.0, 0.0)
    mine = lax.rem(iota((LROWS, TILE), 1), LROWS) == iota((LROWS, TILE), 0)
    sums[...] = jnp.zeros_like(sums)
    for blk in range(here):
        for d in range(3):
            s = dot(acc[blk * 3 + d], seg_sum, exact=True)
            sums[d : d + 1, blk * TILE : (blk + 1) * TILE] = jnp.sum(
                jnp.where(mine, s, 0.0), axis=0, keepdims=True
            )
    hot = one_hot_slots(slots_ref, atom, atoms)
    pair = dot(sums[...], hot, ((1,), (1,)), exact=True)[0:3]
    moved, half, spring = state_ref[0], state_ref[1], state_ref[2]
    force = pair + spring
    pos_out[:, 0, :] = moved
    force_out[:, 0, :] = force
    vel_out[:, 0, :] = half + (0.5 * TIME_STEP) * force / mass_ref[...]


def body(
    positions, velocities, forces_now, masses, features, tile_blocks, block_slots,
    w_basis, w_feat, hidden_bias, w_out,
):
    atoms = positions.shape[2]
    hid, nb = w_basis.shape
    here = atoms // TILE
    shards, beads = lax.axis_size("atom"), lax.axis_size("bead")
    span, first = window(here, shards)
    mass_row = masses.reshape(1, atoms)
    slot_row = block_slots.reshape(1, atoms)
    vmem = pl.BlockSpec(memory_space=pltpu.VMEM)
    rim, state, fwd, bwd, read = pl.pallas_call(
        functools.partial(exchange_kernel, shards, beads, span, first),
        out_shape=(
            jax.ShapeDtypeStruct((span, hid + 16, atoms), bf16),
            jax.ShapeDtypeStruct((3, 3, atoms), f32),
            jax.ShapeDtypeStruct((STACK * hid, STACK * nb), bf16),
            jax.ShapeDtypeStruct((STACK * nb, STACK * hid), bf16),
            jax.ShapeDtypeStruct((16, STACK * hid), bf16),
        ),
        in_specs=[vmem] * 9,
        out_specs=(vmem,) * 5,
        scratch_shapes=[
            pltpu.VMEM((8, atoms), f32),
            pltpu.VMEM((2, 8, atoms), f32),
            pltpu.SemaphoreType.DMA((span,)),
            pltpu.SemaphoreType.DMA((span,)),
            pltpu.SemaphoreType.DMA((2,)),
            pltpu.SemaphoreType.DMA((2,)),
        ],
        compiler_params=pltpu.CompilerParams(collective_id=0, has_side_effects=True),
        name="exchange",
    )(positions, velocities, forces_now, mass_row, features, slot_row, w_feat, w_basis.T, w_out.reshape(1, hid))
    out = jax.ShapeDtypeStruct(positions.shape, f32)
    entries = here * span * here + 2
    return pl.pallas_call(
        functools.partial(pair_kernel, shards, span, first, tile_blocks.shape[1]),
        out_shape=(out, out, out),
        in_specs=[pl.BlockSpec(memory_space=pltpu.SMEM)] + [vmem] * 8,
        out_specs=(vmem, vmem, vmem),
        scratch_shapes=[
            pltpu.VMEM((span * here, 8, TILE), f32),
            pltpu.VMEM((span * here, hid, TILE), f32),
            pltpu.VMEM((here * 3, LROWS, TILE), f32),
            pltpu.VMEM((here * 3, TILE, TILE), f32),
            pltpu.VMEM((here * LROWS, hid, TILE), f32),
            pltpu.VMEM((entries, TILE, TILE), i32),
            pltpu.VMEM((here * 3, LROWS, TILE), f32),
            pltpu.VMEM((8, atoms), f32),
            pltpu.VMEM((2, LROWS, TILE), f32),
            pltpu.VMEM((2, LROWS, TILE), i32),
            pltpu.VMEM((2, LROWS, TILE), f32),
            pltpu.VMEM((2, LROWS, TILE), f32),
            pltpu.SMEM((entries,), i32),
            pltpu.SMEM((entries,), i32),
            pltpu.SMEM((entries,), i32),
            pltpu.SMEM((entries * SEGS + 2,), i32),
        ],
        name="pairs",
    )(
        tile_blocks, rim, state, mass_row, slot_row, fwd, bwd, read,
        hidden_bias.reshape(1, hid),
    )


def solution(mesh):
    vec = P(None, "bead", "atom")
    return jax.shard_map(
        body,
        mesh=mesh,
        in_specs=(
            vec, vec, vec, P("atom"), P("bead", None, "atom"), P("atom", None), P("atom"),
            P(), P(), P(), P(),
        ),
        out_specs=(vec, vec, vec),
        check_vma=False,
    )
```
